512 devices in a mesh: grp: 32 (over z, x_lo, core), dp: 16 (over x_hi, y).
Axes of the slice: x: 4 (x_hi: 2, x_lo: 2; x = x_hi * 2 + x_lo), y: 8, z: 8, core: 2. Of those that a mesh axis runs over, the one named last changes fastest.
Arguments:
- q_rows: bfloat16 [65536, 4096], P(('grp', 'dp')), may hold values from -6 to 6
- k_rows: bfloat16 [65536, 1024], P(('grp', 'dp')), may hold values from -6 to 6
- value_rows: bfloat16 [65536, 1024], P(('grp', 'dp')), may hold values from -6 to 6
- grad_out: bfloat16 [65536, 4096], P(('grp', 'dp')), may hold values from -6 to 6
- lengths: int32 [16, 4, 4], P('dp'), may hold values from 0 to 1024, as said below
- send_rows: int32 [512, 16, 12], P(('grp', 'dp')), may hold values from -1 to 127, as said below
- recv_slots: int32 [16, 4096], P('dp', 'grp'), may hold values from 0 to 191, as said below
Outputs:
- grad_q: bfloat16 [65536, 4096], P(('grp', 'dp'))
- key_gradient: bfloat16 [65536, 1024], P(('grp', 'dp'))
- value_gradient: bfloat16 [65536, 1024], P(('grp', 'dp'))
The draws below stay inside these ranges and needn't reach their ends.
Inputs may be any that keep to these rules, and one draw needn't show every extreme that they name: Entry [e, t] holds the lengths of the sequences packed in order into column (e, t); they sum to 1024, trailing entries are 0, and some column holds a single sequence of 1024. `send_rows`: row g * 16 + d lists for every dp index the local rows that the device of grp index g and dp index d sends there, -1 marking an empty slot; each local row is listed exactly once, and every device fills all 12 slots for some dp index. `recv_slots`: entry [e, P] names the slot d * 12 + c (sender d along dp, its slot c) whose row takes position P on the device of grp index P // 128 and dp index e; every filled slot is named exactly once and no empty one.
All inputs are finite; a program needn't handle non-finite values.
Results may differ from the reference program's by a relative error of at most 0.014.
Values may be sent and summed in bfloat16 or wider, within the bound.
No kernel may reach another device: no remote copies, remote signals or barrier semaphores. Data moves between devices by JAX's collectives and lax.ppermute only.
A program may use at most 128 MiB of HBM per device.

```python
import math
import jax
import jax.numpy as jnp
from jax import lax

QUERY_HEADS = 32
KEY_VALUE_HEADS = 8
HEAD_DIM = 128
TOK_DEV = 128
COLUMN_TOKENS = 1024
MAXLEN = 1024
GROUPS = 4
INDEX_TOKENS = 4096
TOTAL_ROWS = 65536
CAP = 12
SEQS = 4
N_GRP = 32
N_DP = 16


def owner_map_drawn(send_rows, recv_slots):
    columns = send_rows.shape[1]
    place = jnp.arange(INDEX_TOKENS, dtype=jnp.int32) // TOK_DEV
    source = recv_slots // CAP
    within = recv_slots % CAP
    target = jnp.arange(columns, dtype=jnp.int32)[:, None]
    sender = place[None, :] * columns + source
    return sender * TOK_DEV + send_rows[sender, target, within]


def plan_tables(key):
    key = jax.random.fold_in(key, 101)
    base_share = TOK_DEV // N_DP
    extra_rows = base_share // 2

    def one_group(group_key):
        key_shift, key_step, key_order, key_place = jax.random.split(group_key, 4)
        shift_by = jax.random.randint(key_shift, (), 0, N_DP)
        stride = jax.random.randint(key_step, (), 1, N_DP)
        sender = jnp.arange(N_DP)[:, None]
        target = jnp.arange(N_DP)[None, :]
        raised = ((target - sender - shift_by) % N_DP == 0).astype(jnp.int32)
        lowered = ((target - sender - shift_by - stride) % N_DP == 0).astype(jnp.int32)
        counts = base_share + extra_rows * (raised - lowered)
        orders = jax.vmap(lambda subkey: jax.random.permutation(subkey, TOK_DEV))(jax.random.split(key_order, N_DP))
        starts = jnp.cumsum(counts, axis=1) - counts
        slot_ids = jnp.arange(CAP)
        wanted = jnp.clip(starts[:, :, None] + slot_ids[None, None, :], 0, TOK_DEV - 1)
        filled = slot_ids[None, None, :] < counts[:, :, None]
        chosen = jnp.take_along_axis(orders, wanted.reshape(N_DP, N_DP * CAP), axis=1).reshape(N_DP, N_DP, CAP)
        outgoing = jnp.where(filled, chosen, -1)
        filled_in = jnp.transpose(filled, (1, 0, 2)).reshape(N_DP, N_DP * CAP)
        item_ids = jnp.arange(N_DP * CAP)
        ranked = jnp.where(filled_in, item_ids[None, :], item_ids[None, :] + N_DP * CAP)
        firsts = jnp.argsort(ranked, axis=1, stable=True)[:, :TOK_DEV]
        shuffles = jax.vmap(lambda subkey: jax.random.permutation(subkey, TOK_DEV))(jax.random.split(key_place, N_DP))
        receives = jnp.take_along_axis(firsts, shuffles, axis=1)
        return (outgoing, receives)
    outgoing, receives = jax.vmap(one_group)(jax.random.split(key, N_GRP))
    send_rows = outgoing.reshape(N_GRP * N_DP, N_DP, CAP).astype(jnp.int32)
    recv_slots = jnp.transpose(receives, (1, 0, 2)).reshape(N_DP, INDEX_TOKENS).astype(jnp.int32)
    return (send_rows, recv_slots)


def column_lengths(key):
    key = jax.random.fold_in(key, 202)
    key_size, key_flag, key_force = jax.random.split(key, 3)
    drawn_lengths = jax.random.randint(key_size, (N_DP, GROUPS, SEQS), MAXLEN // 4, MAXLEN + 1)
    flags = jax.random.randint(key_flag, (N_DP, GROUPS), 0, 2)
    forced = jax.random.randint(key_force, (), 0, N_DP * GROUPS)
    column_ids = jnp.arange(N_DP * GROUPS).reshape(N_DP, GROUPS)
    full = (flags == 1) | (column_ids == forced)
    first_slot = jnp.arange(SEQS)[None, None, :] == 0
    drawn_lengths = jnp.where(full[:, :, None] & first_slot, MAXLEN, drawn_lengths)
    seq_ends = jnp.minimum(jnp.cumsum(drawn_lengths, axis=2), COLUMN_TOKENS)
    starts = jnp.concatenate([jnp.zeros((N_DP, GROUPS, 1), seq_ends.dtype), seq_ends[:, :, :-1]], 2)
    return (seq_ends - starts).astype(jnp.int32)


def to_owner(row_layout, send_rows, recv_slots):
    owners = owner_map_drawn(send_rows, recv_slots).reshape(-1)
    width = row_layout.shape[2]
    return jnp.zeros((TOTAL_ROWS, width), jnp.float32).at[owners].set(row_layout.reshape(-1, width))


def draw_q_rows(key, part):
    owned_key = jax.random.fold_in(key, 3)
    send_rows, recv_slots = plan_tables(key)
    row_layout = jax.random.truncated_normal(owned_key, -6.0, 6.0, (N_DP, INDEX_TOKENS, QUERY_HEADS * HEAD_DIM), jnp.float32)
    return to_owner(row_layout, send_rows, recv_slots).astype(jnp.bfloat16)


def draw_k_rows(key, part):
    owned_key = jax.random.fold_in(key, 5)
    send_rows, recv_slots = plan_tables(key)
    row_layout = jax.random.truncated_normal(owned_key, -6.0, 6.0, (N_DP, INDEX_TOKENS, KEY_VALUE_HEADS * HEAD_DIM), jnp.float32)
    return to_owner(row_layout, send_rows, recv_slots).astype(jnp.bfloat16)


def draw_lengths(key, part):
    return column_lengths(key)


def draw_send_rows(key, part):
    return plan_tables(key)[0]


def draw_recv_slots(key, part):
    return plan_tables(key)[1]


def shard_levels(key, shape, pieces, smallest, top_value):
    level, own = 1.0, jax.random.fold_in(key, 6)
    for dim, shards_of in pieces:
        draws = jnp.exp(jax.random.uniform(jax.random.fold_in(own, dim), (shards_of,), jnp.float32, smallest / len(pieces), top_value / len(pieces)))
        level = level * jnp.repeat(draws, shape[dim] // shards_of).reshape([-1 if axis == dim else 1 for axis in range(len(shape))])
    return level


def bell_draw(rng, dims, scale, reach, pieces=(), held_as=jnp.bfloat16):
    level = shard_levels(rng, dims, pieces, -0.22, 0.18) if pieces else 1.0
    result = jax.random.normal(rng, dims, jnp.float32) * scale * level
    return jnp.minimum(jnp.maximum(result, -reach), reach).astype(held_as)


def setup_inputs(seed: int = 0) -> dict:
    key_list = jax.random.split(jax.random.key(seed), 8)
    return {
        "q_rows": draw_q_rows(jax.random.fold_in(key_list[7], 71), 0),
        "k_rows": draw_k_rows(jax.random.fold_in(key_list[7], 71), 0),
        "value_rows": bell_draw(key_list[2], (TOTAL_ROWS, KEY_VALUE_HEADS * HEAD_DIM), 1.0, 6.0, ((0, 512),)),
        "grad_out": bell_draw(key_list[3], (TOTAL_ROWS, QUERY_HEADS * HEAD_DIM), 1.0, 6.0, ((0, 512),)),
        "lengths": draw_lengths(jax.random.fold_in(key_list[7], 71), 0),
        "send_rows": draw_send_rows(jax.random.fold_in(key_list[7], 71), 0),
        "recv_slots": draw_recv_slots(jax.random.fold_in(key_list[7], 71), 0),
    }


def owner_map(send_rows, recv_slots):
    columns = send_rows.shape[1]
    place = jnp.arange(INDEX_TOKENS, dtype=jnp.int32) // TOK_DEV
    source = recv_slots // CAP
    within = recv_slots % CAP
    target = jnp.arange(columns, dtype=jnp.int32)[:, None]
    sender = place[None, :] * columns + source
    return (sender * TOK_DEV + send_rows[sender, target, within]).astype(jnp.int32)

def segment_ids(lengths):
    seq_ends = jnp.cumsum(lengths, axis=1, dtype=jnp.int32)
    position = jnp.arange(COLUMN_TOKENS, dtype=jnp.int32)
    return lax.optimization_barrier(jnp.sum((seq_ends[:, None, :] <= position[None, :, None]).astype(jnp.int32), axis=2, dtype=jnp.int32))

def column_grads(query_column, key_column, value_column, output_grad_column, segment):
    per_shared_head = QUERY_HEADS // KEY_VALUE_HEADS
    score_scale = 1.0 / math.sqrt(HEAD_DIM)
    position = jnp.arange(COLUMN_TOKENS, dtype=jnp.int32)
    allowed = (segment[:, None] == segment[None, :]) & (position[None, :] <= position[:, None])
    query_rows = query_column.reshape(COLUMN_TOKENS, KEY_VALUE_HEADS, per_shared_head, HEAD_DIM)
    gradient_list = output_grad_column.reshape(COLUMN_TOKENS, KEY_VALUE_HEADS, per_shared_head, HEAD_DIM)
    key_rows = key_column.reshape(COLUMN_TOKENS, KEY_VALUE_HEADS, HEAD_DIM)
    value_list = value_column.reshape(COLUMN_TOKENS, KEY_VALUE_HEADS, HEAD_DIM)

    def single_head(kv_index):
        query_part = query_rows[:, kv_index].astype(jnp.float32)
        grad_part = gradient_list[:, kv_index].astype(jnp.float32)
        key_part = key_rows[:, kv_index].astype(jnp.float32)
        value_part = value_list[:, kv_index].astype(jnp.float32)
        scores = jnp.einsum('mrd,kd->rmk', query_part, key_part) * score_scale
        scores = jnp.where(allowed[None], scores, -jnp.inf)
        row_max = lax.optimization_barrier(jnp.max(scores, axis=-1, keepdims=True))
        shifted = jnp.exp(scores - row_max)
        row_sum = lax.optimization_barrier(jnp.sum(shifted, axis=-1, keepdims=True))
        weights_b = (shifted / row_sum).astype(jnp.bfloat16)
        weights_f = weights_b.astype(jnp.float32)
        attended = jnp.einsum('rmk,kd->mrd', weights_f, value_part).astype(jnp.bfloat16)
        row_delta = jnp.transpose(lax.optimization_barrier(jnp.sum(grad_part * attended.astype(jnp.float32), axis=-1)), (1, 0))
        d_weights = jnp.einsum('mrd,kd->rmk', grad_part, value_part)
        dscore = (weights_f * (d_weights - row_delta[..., None])).astype(jnp.bfloat16).astype(jnp.float32)
        query_gradient = (jnp.einsum('rmk,kd->mrd', dscore, key_part) * score_scale).astype(jnp.bfloat16)
        key_heads = (jnp.einsum('rmk,mrd->krd', dscore, query_part) * score_scale).astype(jnp.bfloat16)
        value_heads = jnp.einsum('rmk,mrd->krd', weights_f, grad_part).astype(jnp.bfloat16)
        key_total = lax.optimization_barrier(jnp.sum(key_heads.astype(jnp.float32), axis=1)).astype(jnp.bfloat16)
        value_total = lax.optimization_barrier(jnp.sum(value_heads.astype(jnp.float32), axis=1)).astype(jnp.bfloat16)
        return (query_gradient, key_total, value_total)
    query_gradient, key_total, value_total = lax.map(single_head, jnp.arange(KEY_VALUE_HEADS, dtype=jnp.int32))
    dq_col = jnp.transpose(query_gradient, (1, 0, 2, 3)).reshape(COLUMN_TOKENS, QUERY_HEADS * HEAD_DIM)
    key_grad_column = jnp.transpose(key_total, (1, 0, 2)).reshape(COLUMN_TOKENS, KEY_VALUE_HEADS * HEAD_DIM)
    value_grad_column = jnp.transpose(value_total, (1, 0, 2)).reshape(COLUMN_TOKENS, KEY_VALUE_HEADS * HEAD_DIM)
    return (dq_col, key_grad_column, value_grad_column)

def reference(q_rows, k_rows, value_rows, grad_out, lengths, send_rows, recv_slots):
    owners = owner_map(send_rows, recv_slots).reshape(N_DP * GROUPS, COLUMN_TOKENS)
    segment = segment_ids(lengths.reshape(N_DP * GROUPS, SEQS))

    def one_column(column_index):
        picked = owners[column_index]
        return column_grads(q_rows[picked], k_rows[picked], value_rows[picked], grad_out[picked], segment[column_index])
    dq_col, key_grad_column, value_grad_column = lax.map(one_column, jnp.arange(N_DP * GROUPS, dtype=jnp.int32))
    row_places = owners.reshape(-1)
    grad_q = jnp.zeros((TOTAL_ROWS, QUERY_HEADS * HEAD_DIM), jnp.bfloat16).at[row_places].set(dq_col.reshape(-1, QUERY_HEADS * HEAD_DIM))
    key_gradient = jnp.zeros((TOTAL_ROWS, KEY_VALUE_HEADS * HEAD_DIM), jnp.bfloat16).at[row_places].set(key_grad_column.reshape(-1, KEY_VALUE_HEADS * HEAD_DIM))
    value_gradient = jnp.zeros((TOTAL_ROWS, KEY_VALUE_HEADS * HEAD_DIM), jnp.bfloat16).at[row_places].set(value_grad_column.reshape(-1, KEY_VALUE_HEADS * HEAD_DIM))
    return (grad_q, key_gradient, value_gradient)
```

```python
import functools
import math

import jax
import jax.numpy as jnp
from jax import lax
from jax.experimental import pallas as pl
from jax.experimental.pallas import tpu as pltpu
from jax.sharding import Mesh
from jax.sharding import PartitionSpec as P

HEAD = 128
SHARERS = 8
PER = 4
TILE = 256
BF = jnp.bfloat16
F32 = jnp.float32
I32 = jnp.int32
NT = (((1,), (1,)), ((), ()))


def dot(a, b, dims=(((1,), (0,)), ((), ()))):
    return lax.dot_general(a, b, dims, preferred_element_type=F32)


def pack_kernel(places_ref, q_ref, k_ref, v_ref, g_ref, out_ref):
    n, cap2, rows = out_ref.shape[0], out_ref.shape[1] // (PER + 1), q_ref.shape[0]
    slots = n * cap2
    pick = (places_ref[...] == lax.broadcasted_iota(I32, (slots, 2 * rows), 1)).astype(BF)

    def put(pair, block):
        out_ref[:, pair * cap2 : (pair + 1) * cap2, :] = block.reshape(n, cap2, HEAD).astype(BF)

    for pair in range(0, PER, 2):
        lanes = slice(pair * HEAD, (pair + 2) * HEAD)
        both = dot(pick, jnp.concatenate([q_ref[:, lanes], g_ref[:, lanes]], axis=0))
        put(pair, both[:, :HEAD])
        put(pair + 1, both[:, HEAD:])
    put(PER, dot(pick, jnp.concatenate([k_ref[...], v_ref[...]], axis=0)))


def attend_kernel(
    lens_ref, rows_of_ref, lanes_of_ref, in_ref, out_ref,
    q_s, g_s, k_s, v_s, kt_s, dqt_s, dk_s, dv_s,
):
    groups, rows = lanes_of_ref.shape
    n = in_ref.shape[0] // groups
    cap2 = in_ref.shape[1] // (PER + 1)
    cap = cap2 // 2
    slots = n * cap2
    column = groups * rows
    scale = 1.0 / math.sqrt(HEAD)
    log_scale = scale * math.log2(math.e)

    for group in range(groups):
        want = rows_of_ref[:, group : group + 1]
        want = jnp.concatenate([want, want + cap], axis=0)
        pick = (want == lax.broadcasted_iota(I32, (2 * rows, slots), 1)).astype(BF)
        at = slice(group * rows, (group + 1) * rows)
        here = slice(group * n, (group + 1) * n)

        def got(pair):
            return in_ref[here, pair * cap2 : (pair + 1) * cap2, :].reshape(slots, HEAD)

        for pair in range(0, PER, 2):
            both = dot(pick, jnp.concatenate([got(pair), got(pair + 1)], axis=1)).astype(BF)
            q_s[pair, at, :] = both[:rows, :HEAD]
            q_s[pair + 1, at, :] = both[:rows, HEAD:]
            g_s[pair, at, :] = both[rows:, :HEAD]
            g_s[pair + 1, at, :] = both[rows:, HEAD:]
        both = dot(pick, got(PER))
        k_s[at, :] = both[:rows].astype(BF)
        v_s[at, :] = both[rows:].astype(BF)
        kt_s[:, at] = both[:rows].T.astype(BF)

    dk_s[...] = jnp.zeros_like(dk_s)
    dv_s[...] = jnp.zeros_like(dv_s)

    def head_turn(head, carry):
        for tile in range(column // TILE):
            at = slice(tile * TILE, (tile + 1) * TILE)
            seen = (tile + 1) * TILE
            query = q_s[head, at, :]
            grad = g_s[head, at, :]
            place = lax.broadcasted_iota(I32, (1, TILE), 1) + tile * TILE
            begin = jnp.zeros((1, TILE), I32)
            end = jnp.int32(0)
            for j in range(lens_ref.shape[0]):
                end = end + lens_ref[j]
                begin = jnp.where(end <= place, end, begin)
            key_place = lax.broadcasted_iota(I32, (seen, TILE), 0)
            allowed = (key_place >= begin) & (key_place <= place)
            raw = dot(k_s[:seen, :], query, NT)
            raw = jnp.where(allowed, raw, -1e30)
            top = jnp.max(raw, axis=0, keepdims=True)
            shifted = jnp.exp2((raw - top) * log_scale)
            total = jnp.sum(shifted, axis=0, keepdims=True)
            weights = (shifted * (1.0 / total)).astype(BF)
            d_weights = dot(v_s[:seen, :], grad, NT)
            weights_f = weights.astype(F32)
            product = weights_f * d_weights
            delta = jnp.sum(product, axis=0, keepdims=True)
            dscore = (product - weights_f * delta).astype(BF)
            dqt_s[head, :, at] = (dot(kt_s[:, :seen], dscore) * scale).astype(BF)
            dk_s[:seen, :] += dot(dscore, query)
            dv_s[:seen, :] += dot(weights, grad)
        return carry

    lax.fori_loop(0, PER, head_turn, 0)
    dk_b = (dk_s[...] * scale).astype(BF)
    dv_b = dv_s[...].astype(BF)

    for group in range(groups):
        at = slice(group * rows, (group + 1) * rows)
        here = slice(group * n, (group + 1) * n)
        want = lanes_of_ref[group : group + 1, :]
        want = jnp.concatenate([want, want + cap], axis=1)
        drop = (lax.broadcasted_iota(I32, (slots, 2 * rows), 0) == want).astype(BF)

        def put(pair, block):
            out_ref[here, pair * cap2 : (pair + 1) * cap2, :] = block.reshape(n, cap2, HEAD).astype(BF)

        for pair in range(PER // 2):
            put(
                pair,
                dot(
                    drop,
                    jnp.concatenate([dqt_s[2 * pair, :, at], dqt_s[2 * pair + 1, :, at]], axis=1),
                    NT,
                ),
            )
        put(PER // 2, dot(drop, jnp.concatenate([dk_b[at], dv_b[at]], axis=0)))


def settle_kernel(places_ref, in_ref, q_ref, k_ref, v_ref):
    n, cap2, rows = in_ref.shape[0], in_ref.shape[1] // 3, q_ref.shape[0]
    slots = n * cap2
    pick = (places_ref[...] == lax.broadcasted_iota(I32, (2 * rows, slots), 0)).astype(BF)

    def got(pair):
        return in_ref[:, pair * cap2 : (pair + 1) * cap2, :].reshape(slots, HEAD)

    first = dot(pick, jnp.concatenate([got(0), got(1)], axis=1)).astype(BF)
    q_ref[:, :HEAD] = first[:rows, :HEAD]
    q_ref[:, HEAD : 2 * HEAD] = first[rows:, :HEAD]
    q_ref[:, 2 * HEAD : 3 * HEAD] = first[:rows, HEAD:]
    q_ref[:, 3 * HEAD :] = first[rows:, HEAD:]
    last = dot(pick, got(2)).astype(BF)
    k_ref[...] = last[:rows]
    v_ref[...] = last[rows:]


def body(q_rows, k_rows, value_rows, grad_out, lengths, send_rows, recv_slots):
    rows = q_rows.shape[0]
    plan = send_rows[0]
    n, cap = plan.shape
    slots = 2 * n * cap
    column = SHARERS * rows
    params = pltpu.CompilerParams(vmem_limit_bytes=60 * 1024 * 1024)
    both_halves = jnp.concatenate([plan, jnp.where(plan >= 0, plan + rows, -1)], axis=1)

    slot_list = lax.all_gather(recv_slots[0], "gl", axis=0)
    lanes_of = slot_list // cap * (2 * cap) + slot_list % cap
    own_lengths = lengths[0][lax.axis_index("gh")]

    wide = pl.BlockSpec((rows, PER * HEAD), lambda i: (0, i))
    narrow = pl.BlockSpec((rows, HEAD), lambda i: (0, i))
    packed = pl.pallas_call(
        pack_kernel,
        grid=(SHARERS,),
        in_specs=[pl.BlockSpec((slots, 1), lambda i: (0, 0)), wide, narrow, narrow, wide],
        out_specs=pl.BlockSpec((n, (PER + 1) * 2 * cap, HEAD), lambda i: (i, 0, 0)),
        out_shape=jax.ShapeDtypeStruct((SHARERS * n, (PER + 1) * 2 * cap, HEAD), BF),
        compiler_params=params,
        name="pack",
    )(both_halves.reshape(slots, 1), q_rows, k_rows, value_rows, grad_out)
    arrived = lax.all_to_all(packed, ("gl", "dp"), split_axis=0, concat_axis=0, tiled=True)

    vmem = pl.BlockSpec(memory_space=pltpu.VMEM)
    returned = pl.pallas_call(
        attend_kernel,
        in_specs=[pl.BlockSpec(memory_space=pltpu.SMEM), vmem, vmem, vmem],
        out_specs=vmem,
        out_shape=jax.ShapeDtypeStruct((SHARERS * n, 6 * cap, HEAD), BF),
        scratch_shapes=[
            pltpu.VMEM((PER, column, HEAD), BF),
            pltpu.VMEM((PER, column, HEAD), BF),
            pltpu.VMEM((column, HEAD), BF),
            pltpu.VMEM((column, HEAD), BF),
            pltpu.VMEM((HEAD, column), BF),
            pltpu.VMEM((PER, HEAD, column), BF),
            pltpu.VMEM((column, HEAD), F32),
            pltpu.VMEM((column, HEAD), F32),
        ],
        compiler_params=params,
        name="attend",
    )(own_lengths, lanes_of.T, lanes_of, arrived)
    home = lax.all_to_all(returned, ("gl", "dp"), split_axis=0, concat_axis=0, tiled=True)

    return pl.pallas_call(
        settle_kernel,
        grid=(SHARERS,),
        in_specs=[
            pl.BlockSpec((1, slots), lambda i: (0, 0)),
            pl.BlockSpec((n, 6 * cap, HEAD), lambda i: (i, 0, 0)),
        ],
        out_specs=[wide, narrow, narrow],
        out_shape=[
            jax.ShapeDtypeStruct(q_rows.shape, BF),
            jax.ShapeDtypeStruct(k_rows.shape, BF),
            jax.ShapeDtypeStruct(value_rows.shape, BF),
        ],
        compiler_params=params,
        name="settle",
    )(both_halves.reshape(1, slots), home)


def solution(mesh):
    fine = Mesh(mesh.devices.reshape(-1, SHARERS, mesh.devices.shape[1]), ("gh", "gl", "dp"))
    grp = ("gh", "gl")
    rows = P(("gh", "gl", "dp"), None)
    mapped = jax.shard_map(
        body,
        mesh=fine,
        in_specs=(
            rows,
            rows,
            rows,
            rows,
            P("dp", None, None),
            P(("gh", "gl", "dp"), None, None),
            P("dp", grp),
        ),
        out_specs=(rows, rows, rows),
        check_vma=False,
    )
    return lambda *args: tuple(mapped(*args))
```

```python
import math

import jax
import jax.numpy as jnp
from jax import lax
from jax.experimental import pallas as pl
from jax.experimental.pallas import tpu as pltpu
from jax.sharding import Mesh
from jax.sharding import PartitionSpec as P

HEAD = 128
SHARERS = 8
LOW = -1e30
PER = 4
TILE = 256
BF = jnp.bfloat16
F32 = jnp.float32
I32 = jnp.int32
NT = (((1,), (1,)), ((), ()))


def dot(a, b, dims=(((1,), (0,)), ((), ()))):
    return lax.dot_general(a, b, dims, preferred_element_type=F32)


def spread(plan, rows):
    n, cap = plan.shape
    cap2 = 2 * cap
    slots = n * cap2
    both = jnp.concatenate([plan, jnp.where(plan >= 0, plan + rows, -1)], axis=1)
    slot = lax.broadcasted_iota(I32, (slots, n), 0)
    first = lax.broadcasted_iota(I32, (slots, n), 1) * cap2
    owns = (slot >= first) & (slot < first + cap2)
    table = dot(owns.astype(BF), both.astype(F32).astype(BF))
    base = jnp.sum(jnp.where(owns, first, 0), axis=1, keepdims=True)
    within = lax.broadcasted_iota(I32, (slots, cap2), 0) - base
    here = within == lax.broadcasted_iota(I32, (slots, cap2), 1)
    return jnp.sum(jnp.where(here, table, 0.0), axis=1, keepdims=True)


def pack_kernel(
    plan_ref, q_hbm, k_hbm, v_hbm, g_hbm, out_ref, q_s, k_s, v_s, g_s, sems
):
    n, cap = plan_ref.shape
    rows = q_s.shape[0]
    cap2 = 2 * cap
    slots = n * cap2
    pairs = ((q_hbm, q_s), (k_hbm, k_s), (v_hbm, v_s), (g_hbm, g_s))
    copies = []
    for group in range(SHARERS):
        for i, (source, held) in enumerate(pairs):
            width = held.shape[1] // SHARERS
            lanes = pl.ds(group * width, width)
            copies.append(
                pltpu.make_async_copy(source.at[:, lanes], held.at[:, lanes], sems.at[group, i])
            )
            copies[-1].start()
    want = spread(plan_ref[...], rows)
    pick = (want == lax.broadcasted_iota(I32, (slots, 2 * rows), 1).astype(F32)).astype(BF)

    for group in range(SHARERS):
        for copy in copies[group * 4 : group * 4 + 4]:
            copy.wait()

        def put(pair, block):
            out_ref[group * n : (group + 1) * n, pair * cap2 : (pair + 1) * cap2, :] = (
                block.reshape(n, cap2, HEAD).astype(BF)
            )

        for pair in range(0, PER, 2):
            lanes = slice((group * PER + pair) * HEAD, (group * PER + pair + 2) * HEAD)
            both = dot(pick, jnp.concatenate([q_s[:, lanes], g_s[:, lanes]], axis=0))
            put(pair, both[:, :HEAD])
            put(pair + 1, both[:, HEAD:])
        lanes = slice(group * HEAD, (group + 1) * HEAD)
        put(PER, dot(pick, jnp.concatenate([k_s[:, lanes], v_s[:, lanes]], axis=0)))


def attend_kernel(
    lens_ref, rows_of_ref, lanes_of_ref, in_ref, out_ref,
    q_s, g_s, k_s, v_s, kt_s, dqt_s, dk_s, dv_s,
):
    groups, rows = lanes_of_ref.shape
    n = in_ref.shape[0] // groups
    cap2 = in_ref.shape[1] // (PER + 1)
    cap = cap2 // 2
    slots = n * cap2
    column = groups * rows
    scale = 1.0 / math.sqrt(HEAD)
    log_scale = scale * math.log2(math.e)

    for group in range(groups):
        want = rows_of_ref[:, group : group + 1]
        want = jnp.concatenate([want, want + cap], axis=0)
        pick = (want == lax.broadcasted_iota(I32, (2 * rows, slots), 1)).astype(BF)
        at = slice(group * rows, (group + 1) * rows)
        here = slice(group * n, (group + 1) * n)

        def got(pair):
            return in_ref[here, pair * cap2 : (pair + 1) * cap2, :].reshape(slots, HEAD)

        for pair in range(0, PER, 2):
            both = dot(pick, jnp.concatenate([got(pair), got(pair + 1)], axis=1)).astype(BF)
            q_s[pair, at, :] = both[:rows, :HEAD]
            q_s[pair + 1, at, :] = both[:rows, HEAD:]
            g_s[pair, at, :] = both[rows:, :HEAD]
            g_s[pair + 1, at, :] = both[rows:, HEAD:]
        both = dot(pick, got(PER))
        k_s[at, :] = both[:rows].astype(BF)
        v_s[at, :] = both[rows:].astype(BF)
        kt_s[:, at] = both[:rows].T.astype(BF)

    dk_s[...] = jnp.zeros_like(dk_s)
    dv_s[...] = jnp.zeros_like(dv_s)
    key_at = lax.broadcasted_iota(I32, (column, TILE), 0)
    causal = key_at[:TILE] <= lax.broadcasted_iota(I32, (TILE, TILE), 1)

    for tile in range(column // TILE):
        old, seen = tile * TILE, (tile + 1) * TILE
        place = lax.broadcasted_iota(I32, (1, TILE), 1) + old
        begin = jnp.zeros((1, TILE), I32)
        end = jnp.int32(0)
        for j in range(lens_ref.shape[0]):
            end = end + lens_ref[j]
            begin = jnp.where(end <= place, end, begin)

        def masked(raw):
            last = jnp.where((key_at[:TILE] >= begin - old) & causal, raw[old:], LOW)
            if not tile:
                return last
            return jnp.concatenate([jnp.where(key_at[:old] >= begin, raw[:old], LOW), last], axis=0)

        queries = [q_s[head, old:seen, :] for head in range(PER)]
        grads = [g_s[head, old:seen, :] for head in range(PER)]
        raws = [masked(dot(k_s[:seen, :], query, NT)) for query in queries]
        d_weights = [dot(v_s[:seen, :], grad, NT) for grad in grads]
        weights, dscores = [], []
        for head in range(PER):
            top = jnp.max(raws[head], axis=0, keepdims=True)
            shifted = jnp.exp2((raws[head] - top) * log_scale)
            total = jnp.sum(shifted, axis=0, keepdims=True)
            weight = (shifted * (1.0 / total)).astype(BF)
            weight_f = weight.astype(F32)
            delta = jnp.sum(weight_f * d_weights[head], axis=0, keepdims=True)
            dscore = (weight_f * (d_weights[head] - delta)).astype(BF)
            dqt_s[head, :, old:seen] = (dot(kt_s[:, :seen], dscore) * scale).astype(BF)
            weights.append(weight)
            dscores.append(dscore)
        dk_s[:seen, :] += dot(jnp.concatenate(dscores, axis=1), jnp.concatenate(queries, axis=0))
        dv_s[:seen, :] += dot(jnp.concatenate(weights, axis=1), jnp.concatenate(grads, axis=0))

    dk_b = (dk_s[...] * scale).astype(BF)
    dv_b = dv_s[...].astype(BF)

    for group in range(groups):
        at = slice(group * rows, (group + 1) * rows)
        here = slice(group * n, (group + 1) * n)
        want = lanes_of_ref[group : group + 1, :]
        want = jnp.concatenate([want, want + cap], axis=1)
        drop = (lax.broadcasted_iota(I32, (slots, 2 * rows), 0) == want).astype(BF)

        def put(pair, block):
            out_ref[here, pair * cap2 : (pair + 1) * cap2, :] = block.reshape(n, cap2, HEAD).astype(BF)

        for pair in range(PER // 2):
            put(
                pair,
                dot(
                    drop,
                    jnp.concatenate([dqt_s[2 * pair, :, at], dqt_s[2 * pair + 1, :, at]], axis=1),
                    NT,
                ),
            )
        put(PER // 2, dot(drop, jnp.concatenate([dk_b[at], dv_b[at]], axis=0)))


def settle_kernel(places_ref, in_ref, q_hbm, k_hbm, v_hbm, q_s, k_s, v_s, sems):
    n, cap2, rows = in_ref.shape[0] // SHARERS, in_ref.shape[1] // 3, q_s.shape[0]
    slots = n * cap2
    pick = (places_ref[...] == lax.broadcasted_iota(I32, (2 * rows, slots), 0)).astype(BF)
    copies = []
    for group in range(SHARERS):
        here = slice(group * n, (group + 1) * n)

        def got(pair):
            return in_ref[here, pair * cap2 : (pair + 1) * cap2, :].reshape(slots, HEAD)

        first = dot(pick, jnp.concatenate([got(0), got(1)], axis=1)).astype(BF)
        base = group * PER * HEAD
        q_s[:, base : base + HEAD] = first[:rows, :HEAD]
        q_s[:, base + HEAD : base + 2 * HEAD] = first[rows:, :HEAD]
        q_s[:, base + 2 * HEAD : base + 3 * HEAD] = first[:rows, HEAD:]
        q_s[:, base + 3 * HEAD : base + 4 * HEAD] = first[rows:, HEAD:]
        last = dot(pick, got(2)).astype(BF)
        lanes = slice(group * HEAD, (group + 1) * HEAD)
        k_s[:, lanes] = last[:rows]
        v_s[:, lanes] = last[rows:]
        for i, (held, target) in enumerate(((q_s, q_hbm), (k_s, k_hbm), (v_s, v_hbm))):
            width = held.shape[1] // SHARERS
            lanes = pl.ds(group * width, width)
            copies.append(
                pltpu.make_async_copy(held.at[:, lanes], target.at[:, lanes], sems.at[group, i])
            )
            copies[-1].start()
    for copy in copies:
        copy.wait()


VMEM = pl.BlockSpec(memory_space=pltpu.VMEM)
OUTSIDE = pl.BlockSpec(memory_space=pltpu.HBM)


def limit(mib):
    return pltpu.CompilerParams(vmem_limit_bytes=mib * 1024 * 1024)


def pack(plan, q_rows, k_rows, value_rows, grad_out):
    n, cap = plan.shape
    args = (q_rows, k_rows, value_rows, grad_out)
    return pl.pallas_call(
        pack_kernel,
        in_specs=[VMEM] + [OUTSIDE] * 4,
        out_specs=VMEM,
        out_shape=pltpu.VMEM((SHARERS * n, (PER + 1) * 2 * cap, HEAD), BF),
        scratch_shapes=[pltpu.VMEM(a.shape, BF) for a in args]
        + [pltpu.SemaphoreType.DMA((SHARERS, 4))],
        compiler_params=limit(16),
        name="pack",
    )(plan, *(pltpu.with_memory_space_constraint(a, pltpu.HBM) for a in args))


def attend(own_lengths, slot_list, arrived, cap):
    lanes_of = slot_list // cap * (2 * cap) + slot_list % cap
    column = slot_list.size
    return pl.pallas_call(
        attend_kernel,
        in_specs=[pl.BlockSpec(memory_space=pltpu.SMEM), VMEM, VMEM, VMEM],
        out_specs=VMEM,
        out_shape=pltpu.VMEM((arrived.shape[0], 6 * cap, HEAD), BF),
        scratch_shapes=[
            pltpu.VMEM((PER, column, HEAD), BF),
            pltpu.VMEM((PER, column, HEAD), BF),
            pltpu.VMEM((column, HEAD), BF),
            pltpu.VMEM((column, HEAD), BF),
            pltpu.VMEM((HEAD, column), BF),
            pltpu.VMEM((PER, HEAD, column), BF),
            pltpu.VMEM((column, HEAD), F32),
            pltpu.VMEM((column, HEAD), F32),
        ],
        compiler_params=limit(32),
        name="attend",
    )(own_lengths, lanes_of.T, lanes_of, pltpu.with_memory_space_constraint(arrived, pltpu.VMEM))


def settle(plan, rows, home):
    n, cap = plan.shape
    both_halves = jnp.concatenate([plan, jnp.where(plan >= 0, plan + rows, -1)], axis=1)
    outs = [
        jax.ShapeDtypeStruct((rows, SHARERS * width * HEAD), BF) for width in (PER, 1, 1)
    ]
    return pl.pallas_call(
        settle_kernel,
        in_specs=[VMEM, VMEM],
        out_specs=[OUTSIDE] * 3,
        out_shape=outs,
        scratch_shapes=[pltpu.VMEM(a.shape, BF) for a in outs]
        + [pltpu.SemaphoreType.DMA((SHARERS, 3))],
        compiler_params=limit(16),
        name="settle",
    )(both_halves.reshape(1, -1), pltpu.with_memory_space_constraint(home, pltpu.VMEM))


def exchange(bundle):
    return lax.all_to_all(bundle, ("gl", "dp"), split_axis=0, concat_axis=0, tiled=True)


def body(q_rows, k_rows, value_rows, grad_out, lengths, send_rows, recv_slots):
    plan = send_rows[0]
    cap = plan.shape[1]
    slot_list = lax.all_gather(recv_slots[0], "gl", axis=0)
    own_lengths = lengths[0][lax.axis_index("gh")]
    arrived = exchange(pack(plan, q_rows, k_rows, value_rows, grad_out))
    home = exchange(attend(own_lengths, slot_list, arrived, cap))
    return settle(plan, q_rows.shape[0], home)


def solution(mesh):
    fine = Mesh(mesh.devices.reshape(-1, SHARERS, mesh.devices.shape[1]), ("gh", "gl", "dp"))
    grp = ("gh", "gl")
    rows = P(("gh", "gl", "dp"), None)
    mapped = jax.shard_map(
        body,
        mesh=fine,
        in_specs=(
            rows,
            rows,
            rows,
            rows,
            P("dp", None, None),
            P(("gh", "gl", "dp"), None, None),
            P("dp", grp),
        ),
        out_specs=(rows, rows, rows),
        check_vma=False,
    )
    return lambda *args: tuple(mapped(*args))
```

```python
import math

import jax
import jax.numpy as jnp
from jax import lax
from jax.experimental import pallas as pl
from jax.experimental.pallas import tpu as pltpu
from jax.sharding import Mesh
from jax.sharding import PartitionSpec as P

HEAD = 128
SHARERS = 8
CORES = 2
LOW = -1e30
PER = 4
TILE = 256
BF = jnp.bfloat16
F32 = jnp.float32
I32 = jnp.int32
NT = (((1,), (1,)), ((), ()))


def dot(a, b, dims=(((1,), (0,)), ((), ()))):
    return lax.dot_general(a, b, dims, preferred_element_type=F32)


def wanted(plan_ref, rows, along_lanes):
    cap, _, n = plan_ref.shape
    cap2 = 2 * cap
    slots = n * cap2
    axis = 0 if along_lanes else 1

    def iotas(size):
        shape = (size, slots) if along_lanes else (slots, size)
        return lax.broadcasted_iota(I32, shape, axis), lax.broadcasted_iota(I32, shape, 1 - axis)

    target, slot = iotas(n)
    first = target * cap2
    owns = (slot >= first) & (slot < first + cap2)
    plan = plan_ref[:, 0, :].astype(F32).astype(BF)
    hot = owns.astype(BF)
    table = dot(plan, hot) if along_lanes else dot(hot, plan, NT)
    base = jnp.sum(jnp.where(owns, first, 0), axis=axis, keepdims=True)
    entry, slot = iotas(cap)
    within = slot - base
    chosen = (within == entry) | (within == entry + cap)
    value = jnp.sum(jnp.where(chosen, table, 0.0), axis=axis, keepdims=True)
    late = jnp.sum(jnp.where(within == entry + cap, 1.0, 0.0), axis=axis, keepdims=True)
    return jnp.where(value >= 0.0, value + late * rows, -1.0)


def pack_kernel(
    plan_ref, q_hbm, k_hbm, v_hbm, g_hbm, out_hbm, q_s, k_s, v_s, g_s, out_s, sems, out_sems
):
    cap, _, n = plan_ref.shape
    rows = q_s.shape[0]
    cap2 = 2 * cap
    slots = n * cap2
    pairs = ((q_hbm, q_s), (k_hbm, k_s), (v_hbm, v_s), (g_hbm, g_s))
    copies = []
    for group in range(SHARERS):
        for i, (source, held) in enumerate(pairs):
            width = held.shape[1] // SHARERS
            lanes = pl.ds(group * width, width)
            copies.append(
                pltpu.make_async_copy(source.at[:, lanes], held.at[:, lanes], sems.at[group, i])
            )
            copies[-1].start()
    want = wanted(plan_ref, rows, False)
    pick = (want == lax.broadcasted_iota(I32, (slots, 2 * rows), 1).astype(F32)).astype(BF)
    sends = []

    for group in range(SHARERS):
        for copy in copies[group * 4 : group * 4 + 4]:
            copy.wait()

        def put(pair, block):
            out_s[group // CORES, :, group % CORES, pair * cap2 : (pair + 1) * cap2, :] = (
                block.reshape(n, cap2, HEAD).astype(BF)
            )

        for pair in range(0, PER, 2):
            lanes = slice((group * PER + pair) * HEAD, (group * PER + pair + 2) * HEAD)
            both = dot(pick, jnp.concatenate([q_s[:, lanes], g_s[:, lanes]], axis=0))
            put(pair, both[:, :HEAD])
            put(pair + 1, both[:, HEAD:])
        lanes = slice(group * HEAD, (group + 1) * HEAD)
        put(PER, dot(pick, jnp.concatenate([k_s[:, lanes], v_s[:, lanes]], axis=0)))
        block = (group // CORES, slice(None), group % CORES)
        sends.append(
            pltpu.make_async_copy(out_s.at[block], out_hbm.at[block], out_sems.at[group])
        )
        sends[-1].start()
    for send in sends:
        send.wait()


def attend_kernel(
    lens_ref, rows_of_ref, lanes_of_ref, in_ref, out_ref,
    q_s, g_s, k_s, v_s, kt_s, dqt_s, dk_s, dv_s,
):
    groups, rows = lanes_of_ref.shape
    n = in_ref.shape[1]
    cap2 = in_ref.shape[3] // (PER + 1)
    cap = cap2 // 2
    slots = n * cap2
    column = groups * rows
    scale = 1.0 / math.sqrt(HEAD)
    log_scale = scale * math.log2(math.e)

    for group in range(groups):
        want = rows_of_ref[:, group : group + 1]
        want = jnp.concatenate([want, want + cap], axis=0)
        pick = (want == lax.broadcasted_iota(I32, (2 * rows, slots), 1)).astype(BF)
        at = slice(group * rows, (group + 1) * rows)

        def got(pair):
            part = in_ref[group // CORES, :, group % CORES, pair * cap2 : (pair + 1) * cap2, :]
            return part.reshape(slots, HEAD)

        for pair in range(0, PER, 2):
            both = dot(pick, jnp.concatenate([got(pair), got(pair + 1)], axis=1)).astype(BF)
            q_s[pair, at, :] = both[:rows, :HEAD]
            q_s[pair + 1, at, :] = both[:rows, HEAD:]
            g_s[pair, at, :] = both[rows:, :HEAD]
            g_s[pair + 1, at, :] = both[rows:, HEAD:]
        both = dot(pick, got(PER))
        k_s[at, :] = both[:rows].astype(BF)
        v_s[at, :] = both[rows:].astype(BF)
        kt_s[:, at] = both[:rows].T.astype(BF)

    dk_s[...] = jnp.zeros_like(dk_s)
    dv_s[...] = jnp.zeros_like(dv_s)
    key_at = lax.broadcasted_iota(I32, (column, TILE), 0)
    causal = key_at[:TILE] <= lax.broadcasted_iota(I32, (TILE, TILE), 1)

    for tile in range(column // TILE):
        old, seen = tile * TILE, (tile + 1) * TILE
        place = lax.broadcasted_iota(I32, (1, TILE), 1) + old
        begin = jnp.zeros((1, TILE), I32)
        end = jnp.int32(0)
        for j in range(lens_ref.shape[0]):
            end = end + lens_ref[j]
            begin = jnp.where(end <= place, end, begin)

        def masked(raw):
            last = jnp.where((key_at[:TILE] >= begin - old) & causal, raw[old:], LOW)
            if not tile:
                return last
            return jnp.concatenate([jnp.where(key_at[:old] >= begin, raw[:old], LOW), last], axis=0)

        queries = [q_s[head, old:seen, :] for head in range(PER)]
        grads = [g_s[head, old:seen, :] for head in range(PER)]
        raws = [masked(dot(k_s[:seen, :], query, NT)) for query in queries]
        d_weights = [dot(v_s[:seen, :], grad, NT) for grad in grads]
        weights, dscores = [], []
        for head in range(PER):
            top = jnp.max(raws[head], axis=0, keepdims=True)
            shifted = jnp.exp2((raws[head] - top) * log_scale)
            total = jnp.sum(shifted, axis=0, keepdims=True)
            weight = (shifted * (1.0 / total)).astype(BF)
            weight_f = weight.astype(F32)
            delta = jnp.sum(weight_f * d_weights[head], axis=0, keepdims=True)
            dscore = (weight_f * (d_weights[head] - delta)).astype(BF)
            dqt_s[head, :, old:seen] = (dot(kt_s[:, :seen], dscore) * scale).astype(BF)
            weights.append(weight)
            dscores.append(dscore)
        dk_s[:seen, :] += dot(jnp.concatenate(dscores, axis=1), jnp.concatenate(queries, axis=0))
        dv_s[:seen, :] += dot(jnp.concatenate(weights, axis=1), jnp.concatenate(grads, axis=0))

    dk_b = (dk_s[...] * scale).astype(BF)
    dv_b = dv_s[...].astype(BF)

    for group in range(groups):
        at = slice(group * rows, (group + 1) * rows)
        want = lanes_of_ref[group : group + 1, :]
        want = jnp.concatenate([want, want + cap], axis=1)
        drop = (lax.broadcasted_iota(I32, (slots, 2 * rows), 0) == want).astype(BF)

        def put(pair, block):
            out_ref[group // CORES, :, group % CORES, pair * cap2 : (pair + 1) * cap2, :] = (
                block.reshape(n, cap2, HEAD).astype(BF)
            )

        for pair in range(PER // 2):
            put(
                pair,
                dot(
                    drop,
                    jnp.concatenate([dqt_s[2 * pair, :, at], dqt_s[2 * pair + 1, :, at]], axis=1),
                    NT,
                ),
            )
        put(PER // 2, dot(drop, jnp.concatenate([dk_b[at], dv_b[at]], axis=0)))


def settle_kernel(plan_ref, in_ref, q_hbm, k_hbm, v_hbm, q_s, k_s, v_s, sems):
    n, cap2, rows = in_ref.shape[1], in_ref.shape[3] // 3, q_s.shape[0]
    slots = n * cap2
    want = wanted(plan_ref, rows, True)
    pick = (want == lax.broadcasted_iota(I32, (2 * rows, slots), 0).astype(F32)).astype(BF)
    copies = []
    for group in range(SHARERS):

        def got(pair):
            part = in_ref[group // CORES, :, group % CORES, pair * cap2 : (pair + 1) * cap2, :]
            return part.reshape(slots, HEAD)

        first = dot(pick, jnp.concatenate([got(0), got(1)], axis=1)).astype(BF)
        base = group * PER * HEAD
        q_s[:, base : base + HEAD] = first[:rows, :HEAD]
        q_s[:, base + HEAD : base + 2 * HEAD] = first[rows:, :HEAD]
        q_s[:, base + 2 * HEAD : base + 3 * HEAD] = first[:rows, HEAD:]
        q_s[:, base + 3 * HEAD : base + 4 * HEAD] = first[rows:, HEAD:]
        last = dot(pick, got(2)).astype(BF)
        lanes = slice(group * HEAD, (group + 1) * HEAD)
        k_s[:, lanes] = last[:rows]
        v_s[:, lanes] = last[rows:]
        for i, (held, target) in enumerate(((q_s, q_hbm), (k_s, k_hbm), (v_s, v_hbm))):
            width = held.shape[1] // SHARERS
            lanes = pl.ds(group * width, width)
            copies.append(
                pltpu.make_async_copy(held.at[:, lanes], target.at[:, lanes], sems.at[group, i])
            )
            copies[-1].start()
    for copy in copies:
        copy.wait()


VMEM = pl.BlockSpec(memory_space=pltpu.VMEM)
OUTSIDE = pl.BlockSpec(memory_space=pltpu.HBM)


def limit(mib):
    return pltpu.CompilerParams(vmem_limit_bytes=mib * 1024 * 1024)


def pack(plan, q_rows, k_rows, value_rows, grad_out):
    cap, _, n = plan.shape
    args = (q_rows, k_rows, value_rows, grad_out)
    shape = (SHARERS // CORES, n, CORES, (PER + 1) * 2 * cap, HEAD)
    return pl.pallas_call(
        pack_kernel,
        in_specs=[VMEM] + [OUTSIDE] * 4,
        out_specs=OUTSIDE,
        out_shape=pltpu.HBM(shape, BF),
        scratch_shapes=[pltpu.VMEM(a.shape, BF) for a in args]
        + [
            pltpu.VMEM(shape, BF),
            pltpu.SemaphoreType.DMA((SHARERS, 4)),
            pltpu.SemaphoreType.DMA((SHARERS,)),
        ],
        compiler_params=limit(16),
        name="pack",
    )(plan, *(pltpu.with_memory_space_constraint(a, pltpu.HBM) for a in args))


def attend(own_lengths, slot_list, arrived, cap):
    lanes_of = slot_list // cap * (2 * cap) + slot_list % cap
    column = slot_list.size
    return pl.pallas_call(
        attend_kernel,
        in_specs=[pl.BlockSpec(memory_space=pltpu.SMEM), VMEM, VMEM, VMEM],
        out_specs=VMEM,
        out_shape=pltpu.VMEM(arrived.shape[:3] + (6 * cap, HEAD), BF),
        scratch_shapes=[
            pltpu.VMEM((PER, column, HEAD), BF),
            pltpu.VMEM((PER, column, HEAD), BF),
            pltpu.VMEM((column, HEAD), BF),
            pltpu.VMEM((column, HEAD), BF),
            pltpu.VMEM((HEAD, column), BF),
            pltpu.VMEM((PER, HEAD, column), BF),
            pltpu.VMEM((column, HEAD), F32),
            pltpu.VMEM((column, HEAD), F32),
        ],
        compiler_params=limit(32),
        name="attend",
    )(own_lengths, lanes_of.T, lanes_of, arrived)


def settle(plan, rows, home):
    outs = [
        jax.ShapeDtypeStruct((rows, SHARERS * width * HEAD), BF) for width in (PER, 1, 1)
    ]
    return pl.pallas_call(
        settle_kernel,
        in_specs=[VMEM, VMEM],
        out_specs=[OUTSIDE] * 3,
        out_shape=outs,
        scratch_shapes=[pltpu.VMEM(a.shape, BF) for a in outs]
        + [pltpu.SemaphoreType.DMA((SHARERS, 3))],
        compiler_params=limit(16),
        name="settle",
    )(plan, pltpu.with_memory_space_constraint(home, pltpu.VMEM))


def exchange(bundle):
    flat = bundle.reshape((-1,) + bundle.shape[3:])
    return lax.all_to_all(
        flat, ("zx", "dp", "core"), split_axis=0, concat_axis=0, tiled=True
    ).reshape(bundle.shape)


def body(q_rows, k_rows, value_rows, grad_out, lengths, send_rows, recv_slots):
    plan = jnp.transpose(send_rows, (2, 0, 1))
    cap = plan.shape[0]
    slot_list = lax.all_gather(recv_slots[0], ("zx", "core"), axis=0)
    own_lengths = lengths[0][lax.axis_index("gh")]
    arrived = exchange(pack(plan, q_rows, k_rows, value_rows, grad_out))
    home = exchange(attend(own_lengths, slot_list, arrived, cap))
    return settle(plan, q_rows.shape[0], home)


def solution(mesh):
    shape = (-1, SHARERS // CORES, CORES, mesh.devices.shape[1])
    fine = Mesh(mesh.devices.reshape(shape), ("gh", "zx", "core", "dp"))
    grp = ("gh", "zx", "core")
    rows = P(grp + ("dp",), None)
    mapped = jax.shard_map(
        body,
        mesh=fine,
        in_specs=(
            rows,
            rows,
            rows,
            rows,
            P("dp", None, None),
            P(grp + ("dp",), None, None),
            P("dp", grp),
        ),
        out_specs=(rows, rows, rows),
        check_vma=False,
    )
    return lambda *args: tuple(mapped(*args))
```

```python
import math

import jax
import jax.numpy as jnp
from jax import lax
from jax.experimental import pallas as pl
from jax.experimental.pallas import tpu as pltpu
from jax.sharding import Mesh
from jax.sharding import PartitionSpec as P

HEAD = 128
SHARERS = 8
CORES = 2
LOW = -1e30
PER = 4
TILE = 256
BF = jnp.bfloat16
F32 = jnp.float32
I32 = jnp.int32
NT = (((1,), (1,)), ((), ()))


def dot(a, b, dims=(((1,), (0,)), ((), ()))):
    return lax.dot_general(a, b, dims, preferred_element_type=F32)


def wanted(plan_ref, rows, along_lanes):
    cap, _, n = plan_ref.shape
    cap2 = 2 * cap
    slots = n * cap2
    axis = 0 if along_lanes else 1

    def iotas(size):
        shape = (size, slots) if along_lanes else (slots, size)
        return lax.broadcasted_iota(I32, shape, axis), lax.broadcasted_iota(I32, shape, 1 - axis)

    target, slot = iotas(n)
    first = target * cap2
    owns = (slot >= first) & (slot < first + cap2)
    plan = plan_ref[:, 0, :].astype(F32).astype(BF)
    hot = owns.astype(BF)
    table = dot(plan, hot) if along_lanes else dot(hot, plan, NT)
    base = jnp.sum(jnp.where(owns, first, 0), axis=axis, keepdims=True)
    entry, slot = iotas(cap)
    within = slot - base
    chosen = (within == entry) | (within == entry + cap)
    value = jnp.sum(jnp.where(chosen, table, 0.0), axis=axis, keepdims=True)
    late = jnp.sum(jnp.where(within == entry + cap, 1.0, 0.0), axis=axis, keepdims=True)
    return jnp.where(value >= 0.0, value + late * rows, -1.0)


def pack_kernel(
    plan_ref, q_hbm, k_hbm, v_hbm, g_hbm, out_hbm, q_s, k_s, v_s, g_s, out_s, sems, out_sems
):
    cap, _, n = plan_ref.shape
    rows = q_s.shape[0]
    cap2 = 2 * cap
    slots = n * cap2
    pairs = ((q_hbm, q_s), (k_hbm, k_s), (v_hbm, v_s), (g_hbm, g_s))
    copies = []
    for part in range(2):
        for i, (source, held) in enumerate(pairs):
            width = held.shape[1] // 2
            lanes = pl.ds(part * width, width)
            copies.append(
                pltpu.make_async_copy(source.at[:, lanes], held.at[:, lanes], sems.at[part, i])
            )
            copies[-1].start()
    want = wanted(plan_ref, rows, False)
    pick = (want == lax.broadcasted_iota(I32, (slots, 2 * rows), 1).astype(F32)).astype(BF)
    sends = []

    for group in range(SHARERS):
        if group % 4 == 0:
            part = group // 4
            for copy in copies[part * 4 : part * 4 + 4]:
                copy.wait()

        def put(pair, block):
            out_s[group // CORES, :, group % CORES, pair * cap2 : (pair + 1) * cap2, :] = (
                block.reshape(n, cap2, HEAD).astype(BF)
            )

        for pair in range(0, PER, 2):
            lanes = slice((group * PER + pair) * HEAD, (group * PER + pair + 2) * HEAD)
            both = dot(pick, jnp.concatenate([q_s[:, lanes], g_s[:, lanes]], axis=0))
            put(pair, both[:, :HEAD])
            put(pair + 1, both[:, HEAD:])
        lanes = slice(group * HEAD, (group + 1) * HEAD)
        put(PER, dot(pick, jnp.concatenate([k_s[:, lanes], v_s[:, lanes]], axis=0)))
        if group % CORES == CORES - 1:
            block = group // CORES
            sends.append(
                pltpu.make_async_copy(out_s.at[block], out_hbm.at[block], out_sems.at[block])
            )
            sends[-1].start()
    for send in sends:
        send.wait()


def attend_kernel(
    lens_ref, rows_of_ref, lanes_of_ref, in_ref, out_ref,
    q_s, g_s, k_s, v_s, kt_s, dqt_s, dk_s, dv_s,
):
    groups, rows = lanes_of_ref.shape
    n = in_ref.shape[1]
    cap2 = in_ref.shape[3] // (PER + 1)
    cap = cap2 // 2
    slots = n * cap2
    column = groups * rows
    scale = 1.0 / math.sqrt(HEAD)
    log_scale = scale * math.log2(math.e)

    def unpack(group):
        want = rows_of_ref[:, group : group + 1]
        want = jnp.concatenate([want, want + cap], axis=0)
        pick = (want == lax.broadcasted_iota(I32, (2 * rows, slots), 1)).astype(BF)
        at = slice(group * rows, (group + 1) * rows)

        def got(pair):
            part = in_ref[group // CORES, :, group % CORES, pair * cap2 : (pair + 1) * cap2, :]
            return part.reshape(slots, HEAD)

        for pair in range(0, PER, 2):
            both = dot(pick, jnp.concatenate([got(pair), got(pair + 1)], axis=1)).astype(BF)
            q_s[pair, at, :] = both[:rows, :HEAD]
            q_s[pair + 1, at, :] = both[:rows, HEAD:]
            g_s[pair, at, :] = both[rows:, :HEAD]
            g_s[pair + 1, at, :] = both[rows:, HEAD:]
        both = dot(pick, got(PER))
        k_s[at, :] = both[:rows].astype(BF)
        v_s[at, :] = both[rows:].astype(BF)
        kt_s[:, at] = both[:rows].T.astype(BF)

    for group in range(2 * (TILE // rows)):
        unpack(group)

    dk_s[...] = jnp.zeros_like(dk_s)
    dv_s[...] = jnp.zeros_like(dv_s)
    key_at = lax.broadcasted_iota(I32, (column, TILE), 0)
    causal = key_at[:TILE] <= lax.broadcasted_iota(I32, (TILE, TILE), 1)

    def begin_of(tile):
        place = lax.broadcasted_iota(I32, (1, TILE), 1) + tile * TILE
        begin = jnp.zeros((1, TILE), I32)
        end = jnp.int32(0)
        for j in range(lens_ref.shape[0]):
            end = end + lens_ref[j]
            begin = jnp.where(end <= place, end, begin)
        return begin

    def products(tile, head):
        old, seen = tile * TILE, (tile + 1) * TILE
        return (
            dot(k_s[:seen, :], q_s[head, old:seen, :], NT),
            dot(v_s[:seen, :], g_s[head, old:seen, :], NT),
        )

    def softmax(tile, begin, raw, d_weight):
        old = tile * TILE
        last = jnp.where((key_at[:TILE] >= begin - old) & causal, raw[old:], LOW)
        if tile:
            first = jnp.where(key_at[:old] >= begin, raw[:old], LOW)
            raw = jnp.concatenate([first, last], axis=0)
        else:
            raw = last
        top = jnp.max(raw, axis=0, keepdims=True)
        shifted = jnp.exp2((raw - top) * log_scale)
        total = jnp.sum(shifted, axis=0, keepdims=True)
        weight = (shifted * (1.0 / total)).astype(BF)
        weight_f = weight.astype(F32)
        delta = jnp.sum(weight_f * d_weight, axis=0, keepdims=True)
        return weight, (weight_f * (d_weight - delta)).astype(BF)

    def spread_out(total_s, tile, left, right):
        old, seen = tile * TILE, (tile + 1) * TILE
        total_s[:seen, :] += dot(
            jnp.concatenate(left, axis=1),
            jnp.concatenate([right[head, old:seen, :] for head in range(PER)], axis=0),
        )

    tiles = list(range(column // TILE))
    made = [products(tiles[0], head) for head in range(PER)]
    waiting = []
    for step, tile in enumerate(tiles):
        old, seen = tile * TILE, (tile + 1) * TILE
        begin = begin_of(tile)
        following = []
        weights, dscores = [], []
        for head in range(PER):
            if step + 1 < len(tiles) and False:
                following.append(products(tiles[step + 1], head))
            weight, dscore = softmax(tile, begin, *made[head])
            if step + 2 < len(tiles) and head in (0, 2):
                unpack((tile + 2) * TILE // rows + head // 2)
            if step + 1 < len(tiles) and not False:
                following.append(products(tiles[step + 1], head))
            dqt_s[head, :, old:seen] = (dot(kt_s[:, :seen], dscore) * scale).astype(BF)
            weights.append(weight)
            dscores.append(dscore)
            if waiting:
                spread_out(*waiting.pop(0))
        waiting = [(dk_s, tile, dscores, q_s), (dv_s, tile, weights, g_s)]
        if not False:
            for w in waiting:
                spread_out(*w)
            waiting = []
        made = following
    for w in waiting:
        spread_out(*w)

    dk_b = (dk_s[...] * scale).astype(BF)
    dv_b = dv_s[...].astype(BF)

    for group in range(groups):
        at = slice(group * rows, (group + 1) * rows)
        want = lanes_of_ref[group : group + 1, :]
        want = jnp.concatenate([want, want + cap], axis=1)
        drop = (lax.broadcasted_iota(I32, (slots, 2 * rows), 0) == want).astype(BF)

        def put(pair, block):
            out_ref[group // CORES, :, group % CORES, pair * cap2 : (pair + 1) * cap2, :] = (
                block.reshape(n, cap2, HEAD).astype(BF)
            )

        for pair in range(PER // 2):
            put(
                pair,
                dot(
                    drop,
                    jnp.concatenate([dqt_s[2 * pair, :, at], dqt_s[2 * pair + 1, :, at]], axis=1),
                    NT,
                ),
            )
        put(PER // 2, dot(drop, jnp.concatenate([dk_b[at], dv_b[at]], axis=0)))


def settle_kernel(plan_ref, in_ref, q_hbm, k_hbm, v_hbm, q_s, k_s, v_s, sems):
    n, cap2, rows = in_ref.shape[1], in_ref.shape[3] // 3, q_s.shape[0]
    slots = n * cap2
    want = wanted(plan_ref, rows, True)
    pick = (want == lax.broadcasted_iota(I32, (2 * rows, slots), 0).astype(F32)).astype(BF)
    copies = []
    for group in range(SHARERS):

        def got(pair):
            part = in_ref[group // CORES, :, group % CORES, pair * cap2 : (pair + 1) * cap2, :]
            return part.reshape(slots, HEAD)

        first = dot(pick, jnp.concatenate([got(0), got(1)], axis=1)).astype(BF)
        base = group * PER * HEAD
        q_s[:, base : base + HEAD] = first[:rows, :HEAD]
        q_s[:, base + HEAD : base + 2 * HEAD] = first[rows:, :HEAD]
        q_s[:, base + 2 * HEAD : base + 3 * HEAD] = first[:rows, HEAD:]
        q_s[:, base + 3 * HEAD : base + 4 * HEAD] = first[rows:, HEAD:]
        last = dot(pick, got(2)).astype(BF)
        lanes = slice(group * HEAD, (group + 1) * HEAD)
        k_s[:, lanes] = last[:rows]
        v_s[:, lanes] = last[rows:]
        for i, (held, target) in enumerate(((q_s, q_hbm), (k_s, k_hbm), (v_s, v_hbm))):
            width = held.shape[1] // SHARERS
            lanes = pl.ds(group * width, width)
            copies.append(
                pltpu.make_async_copy(held.at[:, lanes], target.at[:, lanes], sems.at[group, i])
            )
            copies[-1].start()
    for copy in copies:
        copy.wait()


VMEM = pl.BlockSpec(memory_space=pltpu.VMEM)
OUTSIDE = pl.BlockSpec(memory_space=pltpu.HBM)


def limit(mib):
    return pltpu.CompilerParams(vmem_limit_bytes=mib * 1024 * 1024)


def pack(plan, q_rows, k_rows, value_rows, grad_out):
    cap, _, n = plan.shape
    args = (q_rows, k_rows, value_rows, grad_out)
    shape = (SHARERS // CORES, n, CORES, (PER + 1) * 2 * cap, HEAD)
    return pl.pallas_call(
        pack_kernel,
        in_specs=[VMEM] + [OUTSIDE] * 4,
        out_specs=OUTSIDE,
        out_shape=pltpu.HBM(shape, BF),
        scratch_shapes=[pltpu.VMEM(a.shape, BF) for a in args]
        + [
            pltpu.VMEM(shape, BF),
            pltpu.SemaphoreType.DMA((SHARERS, 4)),
            pltpu.SemaphoreType.DMA((SHARERS,)),
        ],
        compiler_params=limit(16),
        name="pack",
    )(plan, *(pltpu.with_memory_space_constraint(a, pltpu.HBM) for a in args))


def attend(own_lengths, slot_list, arrived, cap):
    lanes_of = slot_list // cap * (2 * cap) + slot_list % cap
    column = slot_list.size
    return pl.pallas_call(
        attend_kernel,
        in_specs=[pl.BlockSpec(memory_space=pltpu.SMEM), VMEM, VMEM, VMEM],
        out_specs=VMEM,
        out_shape=pltpu.VMEM(arrived.shape[:3] + (6 * cap, HEAD), BF),
        scratch_shapes=[
            pltpu.VMEM((PER, column, HEAD), BF),
            pltpu.VMEM((PER, column, HEAD), BF),
            pltpu.VMEM((column, HEAD), BF),
            pltpu.VMEM((column, HEAD), BF),
            pltpu.VMEM((HEAD, column), BF),
            pltpu.VMEM((PER, HEAD, column), BF),
            pltpu.VMEM((column, HEAD), F32),
            pltpu.VMEM((column, HEAD), F32),
        ],
        compiler_params=limit(32),
        name="attend",
    )(own_lengths, lanes_of.T, lanes_of, arrived)


def settle(plan, rows, home):
    outs = [
        jax.ShapeDtypeStruct((rows, SHARERS * width * HEAD), BF) for width in (PER, 1, 1)
    ]
    return pl.pallas_call(
        settle_kernel,
        in_specs=[VMEM, VMEM],
        out_specs=[OUTSIDE] * 3,
        out_shape=outs,
        scratch_shapes=[pltpu.VMEM(a.shape, BF) for a in outs]
        + [pltpu.SemaphoreType.DMA((SHARERS, 3))],
        compiler_params=limit(16),
        name="settle",
    )(plan, pltpu.with_memory_space_constraint(home, pltpu.VMEM))


def exchange(bundle):
    flat = bundle.reshape((-1,) + bundle.shape[3:])
    return lax.all_to_all(
        flat, ("zx", "dp", "core"), split_axis=0, concat_axis=0, tiled=True
    ).reshape(bundle.shape)


def body(q_rows, k_rows, value_rows, grad_out, lengths, send_rows, recv_slots):
    plan = jnp.transpose(send_rows, (2, 0, 1))
    cap = plan.shape[0]
    slot_list = lax.all_gather(recv_slots[0], ("zx", "core"), axis=0)
    own_lengths = lengths[0][lax.axis_index("gh")]
    arrived = exchange(pack(plan, q_rows, k_rows, value_rows, grad_out))
    home = exchange(attend(own_lengths, slot_list, arrived, cap))
    return settle(plan, q_rows.shape[0], home)


def solution(mesh):
    shape = (-1, SHARERS // CORES, CORES, mesh.devices.shape[1])
    fine = Mesh(mesh.devices.reshape(shape), ("gh", "zx", "core", "dp"))
    grp = ("gh", "zx", "core")
    rows = P(grp + ("dp",), None)
    mapped = jax.shard_map(
        body,
        mesh=fine,
        in_specs=(
            rows,
            rows,
            rows,
            rows,
            P("dp", None, None),
            P(grp + ("dp",), None, None),
            P("dp", grp),
        ),
        out_specs=(rows, rows, rows),
        check_vma=False,
    )
    return lambda *args: tuple(mapped(*args))
```

```python
import math

import jax
import jax.numpy as jnp
from jax import lax
from jax.experimental import pallas as pl
from jax.experimental.pallas import tpu as pltpu
from jax.sharding import Mesh
from jax.sharding import PartitionSpec as P

HEAD = 128
SHARERS = 8
CORES = 2
LOW = -1e30
PER = 4
TILE = 256
BF = jnp.bfloat16
F32 = jnp.float32
I32 = jnp.int32
NT = (((1,), (1,)), ((), ()))


def dot(a, b, dims=(((1,), (0,)), ((), ()))):
    return lax.dot_general(a, b, dims, preferred_element_type=F32)


def wanted(plan_ref, rows, along_lanes):
    cap, _, n = plan_ref.shape
    cap2 = 2 * cap
    slots = n * cap2
    axis = 0 if along_lanes else 1

    def iotas(size):
        shape = (size, slots) if along_lanes else (slots, size)
        return lax.broadcasted_iota(I32, shape, axis), lax.broadcasted_iota(I32, shape, 1 - axis)

    target, slot = iotas(n)
    first = target * cap2
    owns = (slot >= first) & (slot < first + cap2)
    plan = plan_ref[:, 0, :].astype(F32).astype(BF)
    hot = owns.astype(BF)
    table = dot(plan, hot) if along_lanes else dot(hot, plan, NT)
    base = jnp.sum(jnp.where(owns, first, 0), axis=axis, keepdims=True)
    entry, slot = iotas(cap)
    within = slot - base
    chosen = (within == entry) | (within == entry + cap)
    value = jnp.sum(jnp.where(chosen, table, 0.0), axis=axis, keepdims=True)
    late = jnp.sum(jnp.where(within == entry + cap, 1.0, 0.0), axis=axis, keepdims=True)
    return jnp.where(value >= 0.0, value + late * rows, -1.0)


def pack_kernel(
    plan_ref, q_hbm, k_hbm, v_hbm, g_hbm, out_hbm, q_s, k_s, v_s, g_s, out_s, sems, out_sems
):
    cap, _, n = plan_ref.shape
    rows = q_s.shape[0]
    cap2 = 2 * cap
    slots = n * cap2
    pairs = ((q_hbm, q_s), (k_hbm, k_s), (v_hbm, v_s), (g_hbm, g_s))
    copies = []
    for part in range(2):
        for i, (source, held) in enumerate(pairs):
            width = held.shape[1] // 2
            lanes = pl.ds(part * width, width)
            copies.append(
                pltpu.make_async_copy(source.at[:, lanes], held.at[:, lanes], sems.at[part, i])
            )
            copies[-1].start()
    want = wanted(plan_ref, rows, False)
    pick = (want == lax.broadcasted_iota(I32, (slots, 2 * rows), 1).astype(F32)).astype(BF)
    sends = []

    for group in range(SHARERS):
        if group % 4 == 0:
            part = group // 4
            for copy in copies[part * 4 : part * 4 + 4]:
                copy.wait()

        def put(pair, block):
            out_s[group // CORES, :, group % CORES, pair * cap2 : (pair + 1) * cap2, :] = (
                block.reshape(n, cap2, HEAD).astype(BF)
            )

        for pair in range(0, PER, 2):
            lanes = slice((group * PER + pair) * HEAD, (group * PER + pair + 2) * HEAD)
            both = dot(pick, jnp.concatenate([q_s[:, lanes], g_s[:, lanes]], axis=0))
            put(pair, both[:, :HEAD])
            put(pair + 1, both[:, HEAD:])
        lanes = slice(group * HEAD, (group + 1) * HEAD)
        put(PER, dot(pick, jnp.concatenate([k_s[:, lanes], v_s[:, lanes]], axis=0)))
        if group % CORES == CORES - 1:
            block = group // CORES
            sends.append(
                pltpu.make_async_copy(out_s.at[block], out_hbm.at[block], out_sems.at[block])
            )
            sends[-1].start()
    for send in sends:
        send.wait()


def attend_kernel(
    lens_ref, rows_of_ref, lanes_of_ref, in_ref, out_ref,
    q_s, g_s, k_s, v_s, kt_s, dqt_s, dk_s, dv_s,
):
    groups, rows = lanes_of_ref.shape
    n = in_ref.shape[1]
    cap2 = in_ref.shape[3] // (PER + 1)
    cap = cap2 // 2
    slots = n * cap2
    column = groups * rows
    scale = 1.0 / math.sqrt(HEAD)
    log_scale = scale * math.log2(math.e)

    def unpack(group):
        want = rows_of_ref[:, group : group + 1]
        want = jnp.concatenate([want, want + cap], axis=0)
        pick = (want == lax.broadcasted_iota(I32, (2 * rows, slots), 1)).astype(BF)
        at = slice(group * rows, (group + 1) * rows)

        def got(pair):
            part = in_ref[group // CORES, :, group % CORES, pair * cap2 : (pair + 1) * cap2, :]
            return part.reshape(slots, HEAD)

        for pair in range(0, PER, 2):
            both = dot(pick, jnp.concatenate([got(pair), got(pair + 1)], axis=1)).astype(BF)
            q_s[pair, at, :] = both[:rows, :HEAD]
            q_s[pair + 1, at, :] = both[:rows, HEAD:]
            g_s[pair, at, :] = both[rows:, :HEAD]
            g_s[pair + 1, at, :] = both[rows:, HEAD:]
        both = dot(pick, got(PER))
        k_s[at, :] = both[:rows].astype(BF)
        v_s[at, :] = both[rows:].astype(BF)
        kt_s[:, at] = both[:rows].T.astype(BF)

    for group in range(2 * (TILE // rows)):
        unpack(group)

    dk_s[...] = jnp.zeros_like(dk_s)
    dv_s[...] = jnp.zeros_like(dv_s)
    key_at = lax.broadcasted_iota(I32, (column, TILE), 0)
    causal = key_at[:TILE] <= lax.broadcasted_iota(I32, (TILE, TILE), 1)

    def begin_of(tile):
        place = lax.broadcasted_iota(I32, (1, TILE), 1) + tile * TILE
        begin = jnp.zeros((1, TILE), I32)
        end = jnp.int32(0)
        for j in range(lens_ref.shape[0]):
            end = end + lens_ref[j]
            begin = jnp.where(end <= place, end, begin)
        return begin

    def products(tile, head):
        old, seen = tile * TILE, (tile + 1) * TILE
        return (
            dot(k_s[:seen, :], q_s[head, old:seen, :], NT),
            dot(v_s[:seen, :], g_s[head, old:seen, :], NT),
        )

    def softmax(tile, begin, raw, d_weight):
        old = tile * TILE
        last = jnp.where((key_at[:TILE] >= begin - old) & causal, raw[old:], LOW)
        if tile:
            first = jnp.where(key_at[:old] >= begin, raw[:old], LOW)
            raw = jnp.concatenate([first, last], axis=0)
        else:
            raw = last
        top = jnp.max(raw, axis=0, keepdims=True)
        shifted = jnp.exp2((raw - top) * log_scale)
        total = jnp.sum(shifted, axis=0, keepdims=True)
        weight = (shifted * (1.0 / total)).astype(BF)
        weight_f = weight.astype(F32)
        product = weight_f * d_weight
        delta = jnp.sum(product, axis=0, keepdims=True)
        return weight, (product - weight_f * delta).astype(BF)

    def spread_out(total_s, tile, left, right):
        old, seen = tile * TILE, (tile + 1) * TILE
        total_s[:seen, :] += dot(
            jnp.concatenate(left, axis=1),
            jnp.concatenate([right[head, old:seen, :] for head in range(PER)], axis=0),
        )

    tiles = list(range(column // TILE))
    made = [products(tiles[0], head) for head in range(PER)]
    waiting = []
    for step, tile in enumerate(tiles):
        old, seen = tile * TILE, (tile + 1) * TILE
        begin = begin_of(tile)
        following = []
        weights, dscores = [], []
        for head in range(PER):
            if step + 1 < len(tiles) and False:
                following.append(products(tiles[step + 1], head))
            weight, dscore = softmax(tile, begin, *made[head])
            if step + 2 < len(tiles) and head in (0, 2):
                unpack((tile + 2) * TILE // rows + head // 2)
            if step + 1 < len(tiles) and not False:
                following.append(products(tiles[step + 1], head))
            dqt_s[head, :, old:seen] = (dot(kt_s[:, :seen], dscore) * scale).astype(BF)
            weights.append(weight)
            dscores.append(dscore)
            if waiting:
                spread_out(*waiting.pop(0))
        waiting = [(dk_s, tile, dscores, q_s), (dv_s, tile, weights, g_s)]
        if not False:
            for w in waiting:
                spread_out(*w)
            waiting = []
        made = following
    for w in waiting:
        spread_out(*w)

    dk_b = (dk_s[...] * scale).astype(BF)
    dv_b = dv_s[...].astype(BF)

    for group in range(groups):
        at = slice(group * rows, (group + 1) * rows)
        want = lanes_of_ref[group : group + 1, :]
        want = jnp.concatenate([want, want + cap], axis=1)
        drop = (lax.broadcasted_iota(I32, (slots, 2 * rows), 0) == want).astype(BF)

        def put(pair, block):
            out_ref[group // CORES, :, group % CORES, pair * cap2 : (pair + 1) * cap2, :] = (
                block.reshape(n, cap2, HEAD).astype(BF)
            )

        for pair in range(PER // 2):
            put(
                pair,
                dot(
                    drop,
                    jnp.concatenate([dqt_s[2 * pair, :, at], dqt_s[2 * pair + 1, :, at]], axis=1),
                    NT,
                ),
            )
        put(PER // 2, dot(drop, jnp.concatenate([dk_b[at], dv_b[at]], axis=0)))


def settle_kernel(plan_ref, in_ref, q_hbm, k_hbm, v_hbm, q_s, k_s, v_s, sems):
    n, cap2, rows = in_ref.shape[1], in_ref.shape[3] // 3, q_s.shape[0]
    slots = n * cap2
    want = wanted(plan_ref, rows, True)
    pick = (want == lax.broadcasted_iota(I32, (2 * rows, slots), 0).astype(F32)).astype(BF)
    copies = []
    for group in range(SHARERS):

        def got(pair):
            part = in_ref[group // CORES, :, group % CORES, pair * cap2 : (pair + 1) * cap2, :]
            return part.reshape(slots, HEAD)

        first = dot(pick, jnp.concatenate([got(0), got(1)], axis=1)).astype(BF)
        base = group * PER * HEAD
        q_s[:, base : base + HEAD] = first[:rows, :HEAD]
        q_s[:, base + HEAD : base + 2 * HEAD] = first[rows:, :HEAD]
        q_s[:, base + 2 * HEAD : base + 3 * HEAD] = first[:rows, HEAD:]
        q_s[:, base + 3 * HEAD : base + 4 * HEAD] = first[rows:, HEAD:]
        last = dot(pick, got(2)).astype(BF)
        lanes = slice(group * HEAD, (group + 1) * HEAD)
        k_s[:, lanes] = last[:rows]
        v_s[:, lanes] = last[rows:]
        for i, (held, target) in enumerate(((q_s, q_hbm), (k_s, k_hbm), (v_s, v_hbm))):
            width = held.shape[1] // SHARERS
            lanes = pl.ds(group * width, width)
            copies.append(
                pltpu.make_async_copy(held.at[:, lanes], target.at[:, lanes], sems.at[group, i])
            )
            copies[-1].start()
    for copy in copies:
        copy.wait()


VMEM = pl.BlockSpec(memory_space=pltpu.VMEM)
OUTSIDE = pl.BlockSpec(memory_space=pltpu.HBM)


def limit(mib):
    return pltpu.CompilerParams(vmem_limit_bytes=mib * 1024 * 1024)


def pack(plan, q_rows, k_rows, value_rows, grad_out):
    cap, _, n = plan.shape
    args = (q_rows, k_rows, value_rows, grad_out)
    shape = (SHARERS // CORES, n, CORES, (PER + 1) * 2 * cap, HEAD)
    return pl.pallas_call(
        pack_kernel,
        in_specs=[VMEM] + [OUTSIDE] * 4,
        out_specs=OUTSIDE,
        out_shape=pltpu.HBM(shape, BF),
        scratch_shapes=[pltpu.VMEM(a.shape, BF) for a in args]
        + [
            pltpu.VMEM(shape, BF),
            pltpu.SemaphoreType.DMA((SHARERS, 4)),
            pltpu.SemaphoreType.DMA((SHARERS,)),
        ],
        compiler_params=limit(16),
        name="pack",
    )(plan, *(pltpu.with_memory_space_constraint(a, pltpu.HBM) for a in args))


def attend(own_lengths, slot_list, arrived, cap):
    lanes_of = slot_list // cap * (2 * cap) + slot_list % cap
    column = slot_list.size
    return pl.pallas_call(
        attend_kernel,
        in_specs=[pl.BlockSpec(memory_space=pltpu.SMEM), VMEM, VMEM, VMEM],
        out_specs=VMEM,
        out_shape=pltpu.VMEM(arrived.shape[:3] + (6 * cap, HEAD), BF),
        scratch_shapes=[
            pltpu.VMEM((PER, column, HEAD), BF),
            pltpu.VMEM((PER, column, HEAD), BF),
            pltpu.VMEM((column, HEAD), BF),
            pltpu.VMEM((column, HEAD), BF),
            pltpu.VMEM((HEAD, column), BF),
            pltpu.VMEM((PER, HEAD, column), BF),
            pltpu.VMEM((column, HEAD), F32),
            pltpu.VMEM((column, HEAD), F32),
        ],
        compiler_params=limit(32),
        name="attend",
    )(own_lengths, lanes_of.T, lanes_of, arrived)


def settle(plan, rows, home):
    outs = [
        jax.ShapeDtypeStruct((rows, SHARERS * width * HEAD), BF) for width in (PER, 1, 1)
    ]
    return pl.pallas_call(
        settle_kernel,
        in_specs=[VMEM, VMEM],
        out_specs=[OUTSIDE] * 3,
        out_shape=outs,
        scratch_shapes=[pltpu.VMEM(a.shape, BF) for a in outs]
        + [pltpu.SemaphoreType.DMA((SHARERS, 3))],
        compiler_params=limit(16),
        name="settle",
    )(plan, pltpu.with_memory_space_constraint(home, pltpu.VMEM))


def exchange(bundle):
    flat = bundle.reshape((-1,) + bundle.shape[3:])
    return lax.all_to_all(
        flat, ("zx", "dp", "core"), split_axis=0, concat_axis=0, tiled=True
    ).reshape(bundle.shape)


def body(q_rows, k_rows, value_rows, grad_out, lengths, send_rows, recv_slots):
    plan = jnp.transpose(send_rows, (2, 0, 1))
    cap = plan.shape[0]
    slot_list = lax.all_gather(recv_slots[0], ("zx", "core"), axis=0)
    own_lengths = lengths[0][lax.axis_index("gh")]
    arrived = exchange(pack(plan, q_rows, k_rows, value_rows, grad_out))
    home = exchange(attend(own_lengths, slot_list, arrived, cap))
    return settle(plan, q_rows.shape[0], home)


def solution(mesh):
    shape = (-1, SHARERS // CORES, CORES, mesh.devices.shape[1])
    fine = Mesh(mesh.devices.reshape(shape), ("gh", "zx", "core", "dp"))
    grp = ("gh", "zx", "core")
    rows = P(grp + ("dp",), None)
    mapped = jax.shard_map(
        body,
        mesh=fine,
        in_specs=(
            rows,
            rows,
            rows,
            rows,
            P("dp", None, None),
            P(grp + ("dp",), None, None),
            P("dp", grp),
        ),
        out_specs=(rows, rows, rows),
        check_vma=False,
    )
    return lambda *args: tuple(mapped(*args))
```
